32 devices in a mesh: groups: 2 (over y), train: 4 (over z), mat: 2 (over x), sub: 2 (over core).
Axes of the slice: x: 2, y: 2, z: 4, core: 2. Of those that a mesh axis runs over, the one named last changes fastest.
Arguments:
- train_grads: bfloat16 [2048, 8, 4096], P(('groups', 'train'), 'mat'), parts along dimension 0, may hold values from -6 to 6
- test_grads: bfloat16 [4, 56, 8, 4096], P(('groups', 'sub'), 'train', 'mat'), parts along dimension 0, may hold values from -0.03125 to 0.03125
- slab_counts: int32 [8], P(('groups', 'train')), parts along dimension 0, may hold values from 64 to 256, as said below
- test_order: int32 [4, 56], P(('groups', 'sub')), parts along dimension 0, may hold values from 0 to 55, each once within a row
Outputs:
- scores: float32 [2048, 2, 56], P(('groups', 'train', 'mat'), 'sub'), parts along dimension 0
The draws below stay inside these ranges and needn't reach their ends.
There are 2 independent parts, one for each index of `groups`. The reference program is written for one: setup_inputs(seed, part) draws one part's arguments, and reference() takes and returns one part's arrays. A program takes and returns all parts, laid end to end along the dimension named above; each array names one. Nothing has to cross between parts.
Inputs may be any that keep to these rules, and one draw needn't show every extreme that they name: `slab_counts`: each slab block holds between 64 and 256 live rows; some block is full and some holds exactly 64. Each row of test_order is a permutation of 0 to 55.
All inputs are finite; a program needn't handle non-finite values.
Results may differ from the reference program's by a relative error of at most 0.0003.
Values may be sent and summed in bfloat16 or wider, within the bound.
A program may use at most 128 MiB of HBM per device.

```python
import jax
import jax.numpy as jnp

P_SIZE = 4096
MATS = 8
TR_DEV = 256
NTRAIN = 1024
NBLK = 4
NSUBS = 2
TESTS_SUB = 56


def draw_slab_counts(key, part):
    key = jax.random.fold_in(key, 7)
    key_base, key_pick = jax.random.split(key)
    counts = jax.random.randint(key_base, (NBLK,), TR_DEV // 4, TR_DEV + 1)
    picked = jax.random.permutation(key_pick, NBLK)
    counts = counts.at[picked[0]].set(TR_DEV)
    counts = counts.at[picked[1]].set(TR_DEV // 4)
    return counts.astype(jnp.int32)


def level_of(key, dims, cuts, least, largest):
    def one(position, parts):
        heights = jax.random.uniform(jax.random.fold_in(jax.random.fold_in(key, 6), position), (parts,), jnp.float32, least / len(cuts), largest / len(cuts))
        return jnp.repeat(jnp.exp(heights), dims[position] // parts).reshape((-1,) + (1,) * (len(dims) - position - 1))

    level = one(*cuts[0])
    for cut in cuts[1:]:
        level = level * one(*cut)
    return level


def normal_values(own_key, dims, scale, reach, pieces=(), held_as=jnp.bfloat16):
    values = jax.random.normal(own_key, dims, jnp.float32) * scale
    if len(pieces) > 0:
        values = level_of(own_key, dims, pieces, -0.22, 0.18) * values
    return jnp.clip(values, min=-reach, max=reach).astype(held_as)


def setup_inputs(seed: int = 0, part: int = 0) -> dict:
    seeds = jax.random.split(jax.random.key(seed), 5)
    part_keys = jax.random.split(jax.random.fold_in(seeds[4], part), 5)
    train_grads = normal_values(part_keys[0], (NTRAIN, MATS, P_SIZE), 1.0, 6.0, ((0, 4), (1, 2)))
    test_grads = normal_values(part_keys[1], (NSUBS, TESTS_SUB, MATS, P_SIZE), (MATS * P_SIZE) ** -0.5, 0.03125, ((0, 2), (1, 4), (2, 2)))
    slab_counts = draw_slab_counts(jax.random.fold_in(jax.random.fold_in(seeds[4], part), 71), part)
    test_order = jax.vmap(lambda own: jax.random.permutation(own, TESTS_SUB))(jax.random.split(part_keys[3], NSUBS)).reshape((NSUBS, TESTS_SUB)).astype(jnp.int32)
    return {"train_grads": train_grads, "test_grads": test_grads, "slab_counts": slab_counts, "test_order": test_order}


def reference(train_grads, test_grads, slab_counts, test_order):
    flat_train = train_grads.reshape(NTRAIN, MATS * P_SIZE)
    row_index = jnp.arange(NTRAIN)
    live_rows = (row_index % TR_DEV) < slab_counts[row_index // TR_DEV]
    columns = []
    for sub_index in range(NSUBS):
        ordered = test_grads[sub_index].reshape(TESTS_SUB, MATS * P_SIZE)[test_order[sub_index]]
        partial_value = jnp.dot(flat_train, ordered.T, preferred_element_type=jnp.float32)
        columns.append(jnp.where(live_rows[:, None], partial_value, jnp.float32(0.0)))
    return jnp.stack(columns, axis=1)
```

```python
import functools

import jax
import jax.numpy as jnp
from jax import lax
from jax.experimental import pallas as pl
from jax.experimental.pallas import tpu as pltpu
from jax.sharding import PartitionSpec as P

MESH = pl.DeviceIdType.MESH


def kernel(
    n,
    mat_count,
    pieces,
    train_ref,
    test_ref,
    count_ref,
    order_ref,
    out_ref,
    train_in,
    rows_mat,
    tests,
    total,
    outgoing,
    incoming,
    send_sem,
    recv_sem,
    load_sem,
    own_sem,
    out_sem,
    in_sem,
):
    z = lax.axis_index("train")
    mat = lax.axis_index("mat")
    rows, mats, features = train_ref.shape
    held = test_ref.shape[1]
    width = features // pieces
    quarter = rows // mat_count
    columns = out_ref.shape[0]

    barrier = pltpu.get_barrier_semaphore()

    @pl.when(z > 0)
    def _():
        pl.semaphore_signal(barrier, inc=1, device_id={"train": z - 1}, device_id_type=MESH)

    @pl.when(z < n - 1)
    def _():
        pl.semaphore_signal(barrier, inc=1, device_id={"train": z + 1}, device_id_type=MESH)

    for j in range(1, mat_count):
        pl.semaphore_signal(
            barrier, inc=1, device_id={"mat": lax.rem(mat + j, mat_count)}, device_id_type=MESH
        )

    def span(k):
        return pl.ds(pl.multiple_of(k * width, width), width)

    def load_own(k):
        return pltpu.make_async_copy(
            test_ref.at[0, :, :, span(k)], tests.at[z, :, :, span(k)], own_sem.at[k]
        )

    def load_train(k):
        return pltpu.make_async_copy(
            train_ref.at[:, :, span(k)], train_in.at[:, :, span(k)], load_sem.at[k]
        )

    for k in range(pieces):
        load_own(k).start()
        load_train(k).start()

    neighbours = (z > 0).astype(jnp.int32) + (z < n - 1).astype(jnp.int32)
    pl.semaphore_wait(barrier, neighbours + (mat_count - 1))

    def pass_on(src, chunk, k, side):
        return pltpu.make_async_remote_copy(
            src_ref=src,
            dst_ref=tests.at[chunk, :, :, span(k)],
            send_sem=send_sem.at[chunk, side, k],
            recv_sem=recv_sem.at[chunk, k],
            device_id={"train": z - 1 if side == 0 else z + 1},
            device_id_type=MESH,
        )

    def from_own(k, side):
        return pass_on(test_ref.at[0, :, :, span(k)], z, k, side)

    def from_held(chunk, k, side):
        return pass_on(tests.at[chunk, :, :, span(k)], chunk, k, side)

    for k in range(pieces):
        @pl.when(z > 0)
        def _():
            from_own(k, 0).start()

        @pl.when(z < n - 1)
        def _():
            from_own(k, 1).start()

    def close_chunk(chunk, slot, first):
        column_mat = lax.broadcasted_iota(jnp.int32, (rows, held * mats), 1) % mats
        summed = jnp.zeros((rows, held * mats), jnp.float32)
        for m in range(mats):
            strided = slot[pl.ds(m, rows, stride=mats), :]
            summed += jnp.where(column_mat == m, strided, 0.0)
        source = chunk * held + lax.broadcasted_iota(jnp.int32, (held * mats, columns), 0) // mats
        pick = jnp.where(source == order_ref[...], 1.0, 0.0).T
        for j in range(mat_count):
            moved = lax.dot_general(
                pick,
                summed[j * quarter : (j + 1) * quarter],
                (((1,), (1,)), ((), ())),
                precision=lax.Precision.HIGHEST,
                preferred_element_type=jnp.float32,
            )
            if first:
                outgoing[j] = moved
            else:
                outgoing[j] += moved

    left_total, right_total = total.at[0], total.at[1]

    def add(slot, chunk, k):
        block = tests[chunk, :, :, span(k)].reshape(held * mats, width)
        part = lax.dot_general(
            rows_mat[:, span(k)],
            block,
            (((1,), (1,)), ((), ())),
            preferred_element_type=jnp.float32,
        )
        slot[...] = jnp.where(k == 0, 0.0, slot[...]) + part

    def own_piece(k, carry):
        load_train(k).wait()
        rows_mat[:, span(k)] = train_in[:, :, span(k)].reshape(rows * mats, width)
        load_own(k).wait()
        add(left_total, z, k)
        return carry

    lax.fori_loop(0, pieces, own_piece, 0)
    close_chunk(z, left_total, True)

    def hop(d, carry):
        low, high = z - d, z + d

        def piece(k, carry):
            @pl.when(low >= 0)
            def _():
                from_held(low, k, 1).wait_recv()

                @pl.when(z < n - 1)
                def _():
                    from_held(low, k, 1).start()

            @pl.when(high < n)
            def _():
                from_held(high, k, 0).wait_recv()

                @pl.when(z > 0)
                def _():
                    from_held(high, k, 0).start()

            @pl.when(low >= 0)
            def _():
                add(left_total, low, k)

            @pl.when(high < n)
            def _():
                add(right_total, high, k)

            return carry

        lax.fori_loop(0, pieces, piece, 0)

        @pl.when(low >= 0)
        def _():
            close_chunk(low, left_total, False)

        @pl.when(high < n)
        def _():
            close_chunk(high, right_total, False)

        return carry

    lax.fori_loop(1, n, hop, 0)

    def swap(j):
        other = lax.rem(mat + j, mat_count)
        return pltpu.make_async_remote_copy(
            src_ref=outgoing.at[other],
            dst_ref=incoming.at[j],
            send_sem=out_sem.at[j],
            recv_sem=in_sem.at[j],
            device_id={"mat": other},
            device_id_type=MESH,
        )

    for j in range(1, mat_count):
        swap(j).start()
    score = outgoing[mat]
    for j in range(1, mat_count):
        swap(j).wait()
        score += incoming[j]
    place = mat * quarter + lax.broadcasted_iota(jnp.int32, (columns, quarter), 1)
    out_ref[...] = jnp.where(place < count_ref[0], score, 0.0)

    def drain(k, carry):
        @pl.when(z > 0)
        def _():
            from_own(k, 0).wait_send()

        @pl.when(z < n - 1)
        def _():
            from_own(k, 1).wait_send()

        def drain_hop(d, carry):
            @pl.when((z - d >= 0) & (z < n - 1))
            def _():
                from_held(z - d, k, 1).wait_send()

            @pl.when((z + d < n) & (z > 0))
            def _():
                from_held(z + d, k, 0).wait_send()

            return carry

        return lax.fori_loop(1, n, drain_hop, carry)

    lax.fori_loop(0, pieces, drain, 0)


def solution(mesh):
    n = mesh.shape["train"]
    mat_count = mesh.shape["mat"]
    pieces = 4

    def shards(train_grads, test_grads, slab_counts, test_order):
        rows, mats, features = train_grads.shape
        held = test_grads.shape[1]
        columns = test_order.shape[1]
        quarter = rows // mat_count
        any_space = pl.BlockSpec(memory_space=pl.ANY)
        found = pl.pallas_call(
            functools.partial(kernel, n, mat_count, pieces),
            out_shape=jax.ShapeDtypeStruct((columns, quarter), jnp.float32),
            in_specs=[
                any_space,
                any_space,
                pl.BlockSpec(memory_space=pltpu.SMEM),
                pl.BlockSpec(memory_space=pltpu.VMEM),
            ],
            out_specs=pl.BlockSpec(memory_space=pltpu.VMEM),
            scratch_shapes=[
                pltpu.VMEM((rows, mats, features), jnp.bfloat16),
                pltpu.VMEM((rows * mats, features), jnp.bfloat16),
                pltpu.VMEM((n, held, mats, features), jnp.bfloat16),
                pltpu.VMEM((2, rows * mats, held * mats), jnp.float32),
                pltpu.VMEM((mat_count, columns, quarter), jnp.float32),
                pltpu.VMEM((mat_count, columns, quarter), jnp.float32),
                pltpu.SemaphoreType.DMA((n, 2, pieces)),
                pltpu.SemaphoreType.DMA((n, pieces)),
                pltpu.SemaphoreType.DMA((pieces,)),
                pltpu.SemaphoreType.DMA((pieces,)),
                pltpu.SemaphoreType.DMA((mat_count,)),
                pltpu.SemaphoreType.DMA((mat_count,)),
            ],
            compiler_params=pltpu.CompilerParams(
                collective_id=0, has_side_effects=True, vmem_limit_bytes=56 * 1024 * 1024
            ),
        )(train_grads, test_grads, slab_counts, test_order)
        return found.T[:, None, :]

    placed = (
        P(("groups", "train"), "mat", None),
        P(("groups", "sub"), "train", "mat", None),
        P(("groups", "train")),
        P(("groups", "sub"), None),
    )
    return jax.shard_map(
        shards,
        mesh=mesh,
        in_specs=placed,
        out_specs=P(("groups", "train", "mat"), "sub", None),
        check_vma=False,
    )
```

```python
import functools

import jax
import jax.numpy as jnp
from jax import lax
from jax.experimental import pallas as pl
from jax.experimental.pallas import tpu as pltpu
from jax.sharding import PartitionSpec as P

MESH = pl.DeviceIdType.MESH


def kernel(
    n,
    mat_count,
    pieces,
    train_ref,
    test_ref,
    count_ref,
    order_ref,
    out_ref,
    train_in,
    rows_mat,
    tests,
    total,
    outgoing,
    incoming,
    send_sem,
    recv_sem,
    load_sem,
    own_sem,
    out_sem,
    in_sem,
):
    z = lax.axis_index("train")
    mat = lax.axis_index("mat")
    rows, mats, features = train_ref.shape
    held = test_ref.shape[1]
    width = features // pieces
    quarter = rows // mat_count
    columns = out_ref.shape[0]

    barrier = pltpu.get_barrier_semaphore()

    @pl.when(z > 0)
    def _():
        pl.semaphore_signal(barrier, inc=1, device_id={"train": z - 1}, device_id_type=MESH)

    @pl.when(z < n - 1)
    def _():
        pl.semaphore_signal(barrier, inc=1, device_id={"train": z + 1}, device_id_type=MESH)

    for j in range(1, mat_count):
        pl.semaphore_signal(
            barrier, inc=1, device_id={"mat": lax.rem(mat + j, mat_count)}, device_id_type=MESH
        )

    def span(k):
        return pl.ds(pl.multiple_of(k * width, width), width)

    def load_own(k):
        return pltpu.make_async_copy(
            test_ref.at[0, :, :, span(k)], tests.at[z, :, :, span(k)], own_sem.at[k]
        )

    def load_train(k):
        return pltpu.make_async_copy(
            train_ref.at[:, :, span(k)], train_in.at[:, :, span(k)], load_sem.at[k]
        )

    for k in range(pieces):
        load_own(k).start()
        load_train(k).start()

    neighbours = (z > 0).astype(jnp.int32) + (z < n - 1).astype(jnp.int32)
    pl.semaphore_wait(barrier, neighbours + (mat_count - 1))

    def pass_on(src, chunk, k, side):
        return pltpu.make_async_remote_copy(
            src_ref=src,
            dst_ref=tests.at[chunk, :, :, span(k)],
            send_sem=send_sem.at[chunk, side, k],
            recv_sem=recv_sem.at[chunk, k],
            device_id={"train": z - 1 if side == 0 else z + 1},
            device_id_type=MESH,
        )

    def from_own(k, side):
        return pass_on(test_ref.at[0, :, :, span(k)], z, k, side)

    def from_held(chunk, k, side):
        return pass_on(tests.at[chunk, :, :, span(k)], chunk, k, side)

    for k in range(pieces):
        @pl.when((z > 0) & (z < n - 1 - z))
        def _():
            from_own(k, 0).start()

        @pl.when((z < n - 1) & (z >= n - 1 - z))
        def _():
            from_own(k, 1).start()

    for k in range(pieces):
        @pl.when((z > 0) & (z >= n - 1 - z))
        def _():
            from_own(k, 0).start()

        @pl.when((z < n - 1) & (z < n - 1 - z))
        def _():
            from_own(k, 1).start()

    def close_chunk(chunk, slot, first):
        column_mat = lax.broadcasted_iota(jnp.int32, (rows, held * mats), 1) % mats
        summed = jnp.zeros((rows, held * mats), jnp.float32)
        for m in range(mats):
            strided = slot[pl.ds(m, rows, stride=mats), :]
            summed += jnp.where(column_mat == m, strided, 0.0)
        source = chunk * held + lax.broadcasted_iota(jnp.int32, (held * mats, columns), 0) // mats
        pick = jnp.where(source == order_ref[...], 1.0, 0.0).T
        for j in range(mat_count):
            moved = lax.dot_general(
                pick,
                summed[j * quarter : (j + 1) * quarter],
                (((1,), (1,)), ((), ())),
                precision=lax.Precision.HIGHEST,
                preferred_element_type=jnp.float32,
            )
            if first:
                outgoing[j] = moved
            else:
                outgoing[j] += moved

    left_total, right_total, own_total = total.at[0], total.at[1], total.at[2]

    def add(slot, chunk, k):
        block = tests[chunk, :, :, span(k)].reshape(held * mats, width)
        part = lax.dot_general(
            rows_mat[:, span(k)],
            block,
            (((1,), (1,)), ((), ())),
            preferred_element_type=jnp.float32,
        )
        slot[...] = jnp.where(k == 0, 0.0, slot[...]) + part

    def own_piece(k):
        load_train(k).wait()
        rows_mat[:, span(k)] = train_in[:, :, span(k)].reshape(rows * mats, width)
        load_own(k).wait()
        add(own_total, z, k)

    outgoing[...] = jnp.zeros_like(outgoing)

    def hop(d, carry):
        low, high = z - d, z + d

        def piece(k, carry):
            @pl.when(low >= 0)
            def _():
                from_held(low, k, 1).wait_recv()

                @pl.when(z < n - 1)
                def _():
                    from_held(low, k, 1).start()

            @pl.when(high < n)
            def _():
                from_held(high, k, 0).wait_recv()

                @pl.when(z > 0)
                def _():
                    from_held(high, k, 0).start()

            @pl.when(d == 1)
            def _():
                own_piece(k)

            @pl.when(low >= 0)
            def _():
                add(left_total, low, k)

            @pl.when(high < n)
            def _():
                add(right_total, high, k)

            return carry

        lax.fori_loop(0, pieces, piece, 0)

        @pl.when(d == 1)
        def _():
            close_chunk(z, own_total, False)

        @pl.when(low >= 0)
        def _():
            close_chunk(low, left_total, False)

        @pl.when(high < n)
        def _():
            close_chunk(high, right_total, False)

        return carry

    lax.fori_loop(1, n, hop, 0)

    def swap(j):
        other = lax.rem(mat + j, mat_count)
        return pltpu.make_async_remote_copy(
            src_ref=outgoing.at[other],
            dst_ref=incoming.at[j],
            send_sem=out_sem.at[j],
            recv_sem=in_sem.at[j],
            device_id={"mat": other},
            device_id_type=MESH,
        )

    for j in range(1, mat_count):
        swap(j).start()
    score = outgoing[mat]
    for j in range(1, mat_count):
        swap(j).wait()
        score += incoming[j]
    place = mat * quarter + lax.broadcasted_iota(jnp.int32, (columns, quarter), 1)
    out_ref[...] = jnp.where(place < count_ref[0], score, 0.0)

    def drain(k, carry):
        @pl.when(z > 0)
        def _():
            from_own(k, 0).wait_send()

        @pl.when(z < n - 1)
        def _():
            from_own(k, 1).wait_send()

        def drain_hop(d, carry):
            @pl.when((z - d >= 0) & (z < n - 1))
            def _():
                from_held(z - d, k, 1).wait_send()

            @pl.when((z + d < n) & (z > 0))
            def _():
                from_held(z + d, k, 0).wait_send()

            return carry

        return lax.fori_loop(1, n, drain_hop, carry)

    lax.fori_loop(0, pieces, drain, 0)


def solution(mesh):
    n = mesh.shape["train"]
    mat_count = mesh.shape["mat"]
    pieces = 4

    def shards(train_grads, test_grads, slab_counts, test_order):
        rows, mats, features = train_grads.shape
        held = test_grads.shape[1]
        columns = test_order.shape[1]
        quarter = rows // mat_count
        any_space = pl.BlockSpec(memory_space=pl.ANY)
        found = pl.pallas_call(
            functools.partial(kernel, n, mat_count, pieces),
            out_shape=jax.ShapeDtypeStruct((columns, quarter), jnp.float32),
            in_specs=[
                any_space,
                any_space,
                pl.BlockSpec(memory_space=pltpu.SMEM),
                pl.BlockSpec(memory_space=pltpu.VMEM),
            ],
            out_specs=pl.BlockSpec(memory_space=pltpu.VMEM),
            scratch_shapes=[
                pltpu.VMEM((rows, mats, features), jnp.bfloat16),
                pltpu.VMEM((rows * mats, features), jnp.bfloat16),
                pltpu.VMEM((n, held, mats, features), jnp.bfloat16),
                pltpu.VMEM((3, rows * mats, held * mats), jnp.float32),
                pltpu.VMEM((mat_count, columns, quarter), jnp.float32),
                pltpu.VMEM((mat_count, columns, quarter), jnp.float32),
                pltpu.SemaphoreType.DMA((n, 2, pieces)),
                pltpu.SemaphoreType.DMA((n, pieces)),
                pltpu.SemaphoreType.DMA((pieces,)),
                pltpu.SemaphoreType.DMA((pieces,)),
                pltpu.SemaphoreType.DMA((mat_count,)),
                pltpu.SemaphoreType.DMA((mat_count,)),
            ],
            compiler_params=pltpu.CompilerParams(
                collective_id=0, has_side_effects=True, vmem_limit_bytes=56 * 1024 * 1024
            ),
        )(train_grads, test_grads, slab_counts, test_order)
        return found.T[:, None, :]

    placed = (
        P(("groups", "train"), "mat", None),
        P(("groups", "sub"), "train", "mat", None),
        P(("groups", "train")),
        P(("groups", "sub"), None),
    )
    return jax.shard_map(
        shards,
        mesh=mesh,
        in_specs=placed,
        out_specs=P(("groups", "train", "mat"), "sub", None),
        check_vma=False,
    )
```

```python
import functools

import jax
import jax.numpy as jnp
from jax import lax
from jax.experimental import pallas as pl
from jax.experimental.pallas import tpu as pltpu
from jax.sharding import PartitionSpec as P

MESH = pl.DeviceIdType.MESH


def kernel(
    n,
    mat_count,
    pieces,
    train_ref,
    test_ref,
    count_ref,
    order_ref,
    out_ref,
    train_in,
    rows_mat,
    tests,
    total,
    outgoing,
    incoming,
    send_sem,
    recv_sem,
    load_sem,
    own_sem,
    out_sem,
    in_sem,
):
    z = lax.axis_index("train")
    mat = lax.axis_index("mat")
    rows, mats, features = train_ref.shape
    held = test_ref.shape[1]
    width = features // pieces
    quarter = rows // mat_count
    columns = out_ref.shape[0]

    barrier = pltpu.get_barrier_semaphore()

    @pl.when(z > 0)
    def _():
        pl.semaphore_signal(barrier, inc=1, device_id={"train": z - 1}, device_id_type=MESH)

    @pl.when(z < n - 1)
    def _():
        pl.semaphore_signal(barrier, inc=1, device_id={"train": z + 1}, device_id_type=MESH)

    for j in range(1, mat_count):
        pl.semaphore_signal(
            barrier, inc=1, device_id={"mat": lax.rem(mat + j, mat_count)}, device_id_type=MESH
        )

    def span(k):
        return pl.ds(pl.multiple_of(k * width, width), width)

    def load_own(k):
        return pltpu.make_async_copy(
            test_ref.at[0, :, :, span(k)], tests.at[z, :, :, span(k)], own_sem.at[k]
        )

    def load_train(k):
        return pltpu.make_async_copy(
            train_ref.at[:, :, span(k)], train_in.at[:, :, span(k)], load_sem.at[k]
        )

    for k in range(pieces):
        load_own(k).start()
        load_train(k).start()

    neighbours = (z > 0).astype(jnp.int32) + (z < n - 1).astype(jnp.int32)
    pl.semaphore_wait(barrier, neighbours + (mat_count - 1))

    def pass_on(src, chunk, k, side):
        return pltpu.make_async_remote_copy(
            src_ref=src,
            dst_ref=tests.at[chunk, :, :, span(k)],
            send_sem=send_sem.at[chunk, side, k],
            recv_sem=recv_sem.at[chunk, k],
            device_id={"train": z - 1 if side == 0 else z + 1},
            device_id_type=MESH,
        )

    def from_own(k, side):
        return pass_on(test_ref.at[0, :, :, span(k)], z, k, side)

    def from_held(chunk, k, side):
        return pass_on(tests.at[chunk, :, :, span(k)], chunk, k, side)

    for k in range(pieces):
        @pl.when((z > 0) & (z < n - 1 - z))
        def _():
            from_own(k, 0).start()

        @pl.when((z < n - 1) & (z >= n - 1 - z))
        def _():
            from_own(k, 1).start()

    for k in range(pieces):
        @pl.when((z > 0) & (z >= n - 1 - z))
        def _():
            from_own(k, 0).start()

        @pl.when((z < n - 1) & (z < n - 1 - z))
        def _():
            from_own(k, 1).start()

    def close_chunk(chunk, slot, first):
        column_mat = lax.broadcasted_iota(jnp.int32, (rows, held * mats), 1) % mats
        summed = jnp.zeros((rows, held * mats), jnp.float32)
        for m in range(mats):
            strided = slot[pl.ds(m, rows, stride=mats), :]
            summed += jnp.where(column_mat == m, strided, 0.0)
        source = chunk * held + lax.broadcasted_iota(jnp.int32, (held * mats, columns), 0) // mats
        pick = jnp.where(source == order_ref[...], 1.0, 0.0).T.astype(jnp.bfloat16)
        high = summed.astype(jnp.bfloat16)
        rest = summed - high.astype(jnp.float32)
        middle = rest.astype(jnp.bfloat16)
        low = (rest - middle.astype(jnp.float32)).astype(jnp.bfloat16)
        for j in range(mat_count):
            moved = jnp.zeros((columns, quarter), jnp.float32)
            for part in (low, middle, high):
                moved += lax.dot_general(
                    pick,
                    part[j * quarter : (j + 1) * quarter],
                    (((1,), (1,)), ((), ())),
                    preferred_element_type=jnp.float32,
                )
            if first:
                outgoing[j] = moved
            else:
                outgoing[j] += moved

    left_total, right_total, own_total = total.at[0], total.at[1], total.at[2]

    def add(slot, chunk, k):
        block = tests[chunk, :, :, span(k)].reshape(held * mats, width)
        part = lax.dot_general(
            rows_mat[:, span(k)],
            block,
            (((1,), (1,)), ((), ())),
            preferred_element_type=jnp.float32,
        )
        slot[...] = jnp.where(k == 0, 0.0, slot[...]) + part

    def own_piece(k):
        load_train(k).wait()
        rows_mat[:, span(k)] = train_in[:, :, span(k)].reshape(rows * mats, width)
        load_own(k).wait()
        add(own_total, z, k)

    outgoing[...] = jnp.zeros_like(outgoing)

    def hop(d, carry):
        low, high = z - d, z + d

        def piece(k, carry):
            @pl.when(low >= 0)
            def _():
                from_held(low, k, 1).wait_recv()

                @pl.when(z < n - 1)
                def _():
                    from_held(low, k, 1).start()

            @pl.when(high < n)
            def _():
                from_held(high, k, 0).wait_recv()

                @pl.when(z > 0)
                def _():
                    from_held(high, k, 0).start()

            @pl.when(d == 1)
            def _():
                own_piece(k)

            @pl.when(low >= 0)
            def _():
                add(left_total, low, k)

            @pl.when(high < n)
            def _():
                add(right_total, high, k)

            return carry

        lax.fori_loop(0, pieces, piece, 0)

        @pl.when(d == 1)
        def _():
            close_chunk(z, own_total, False)

        @pl.when(low >= 0)
        def _():
            close_chunk(low, left_total, False)

        @pl.when(high < n)
        def _():
            close_chunk(high, right_total, False)

        return carry

    lax.fori_loop(1, n, hop, 0)

    def swap(j):
        other = lax.rem(mat + j, mat_count)
        return pltpu.make_async_remote_copy(
            src_ref=outgoing.at[other],
            dst_ref=incoming.at[j],
            send_sem=out_sem.at[j],
            recv_sem=in_sem.at[j],
            device_id={"mat": other},
            device_id_type=MESH,
        )

    for j in range(1, mat_count):
        swap(j).start()
    score = outgoing[mat]
    for j in range(1, mat_count):
        swap(j).wait()
        score += incoming[j]
    place = mat * quarter + lax.broadcasted_iota(jnp.int32, (columns, quarter), 1)
    out_ref[...] = jnp.where(place < count_ref[0], score, 0.0)

    def drain(k, carry):
        @pl.when(z > 0)
        def _():
            from_own(k, 0).wait_send()

        @pl.when(z < n - 1)
        def _():
            from_own(k, 1).wait_send()

        def drain_hop(d, carry):
            @pl.when((z - d >= 0) & (z < n - 1))
            def _():
                from_held(z - d, k, 1).wait_send()

            @pl.when((z + d < n) & (z > 0))
            def _():
                from_held(z + d, k, 0).wait_send()

            return carry

        return lax.fori_loop(1, n, drain_hop, carry)

    lax.fori_loop(0, pieces, drain, 0)


def solution(mesh):
    n = mesh.shape["train"]
    mat_count = mesh.shape["mat"]
    pieces = 4

    def shards(train_grads, test_grads, slab_counts, test_order):
        rows, mats, features = train_grads.shape
        held = test_grads.shape[1]
        columns = test_order.shape[1]
        quarter = rows // mat_count
        any_space = pl.BlockSpec(memory_space=pl.ANY)
        found = pl.pallas_call(
            functools.partial(kernel, n, mat_count, pieces),
            out_shape=jax.ShapeDtypeStruct((columns, quarter), jnp.float32),
            in_specs=[
                any_space,
                any_space,
                pl.BlockSpec(memory_space=pltpu.SMEM),
                pl.BlockSpec(memory_space=pltpu.VMEM),
            ],
            out_specs=pl.BlockSpec(memory_space=pltpu.VMEM),
            scratch_shapes=[
                pltpu.VMEM((rows, mats, features), jnp.bfloat16),
                pltpu.VMEM((rows * mats, features), jnp.bfloat16),
                pltpu.VMEM((n, held, mats, features), jnp.bfloat16),
                pltpu.VMEM((3, rows * mats, held * mats), jnp.float32),
                pltpu.VMEM((mat_count, columns, quarter), jnp.float32),
                pltpu.VMEM((mat_count, columns, quarter), jnp.float32),
                pltpu.SemaphoreType.DMA((n, 2, pieces)),
                pltpu.SemaphoreType.DMA((n, pieces)),
                pltpu.SemaphoreType.DMA((pieces,)),
                pltpu.SemaphoreType.DMA((pieces,)),
                pltpu.SemaphoreType.DMA((mat_count,)),
                pltpu.SemaphoreType.DMA((mat_count,)),
            ],
            compiler_params=pltpu.CompilerParams(
                collective_id=0, has_side_effects=True, vmem_limit_bytes=56 * 1024 * 1024
            ),
        )(train_grads, test_grads, slab_counts, test_order)
        return found.T[:, None, :]

    placed = (
        P(("groups", "train"), "mat", None),
        P(("groups", "sub"), "train", "mat", None),
        P(("groups", "train")),
        P(("groups", "sub"), None),
    )
    return jax.shard_map(
        shards,
        mesh=mesh,
        in_specs=placed,
        out_specs=P(("groups", "train", "mat"), "sub", None),
        check_vma=False,
    )
```
